32 devices in a mesh: dp: 8 (over z, x), seq: 4 (over y, core).
Axes of the slice: x: 2, y: 2, z: 4, core: 2. Of those that a mesh axis runs over, the one named last changes fastest.
Arguments:
- output_gradient: bfloat16 [6144, 8192], P('dp'), may hold values from -6 to 6
- frozen_down_weight: bfloat16 [14336, 8192], P('seq', 'dp'), may hold values from -0.046875 to 0.046875
- adapter_first_factor: bfloat16 [14336, 64], P('seq'), may hold values from -0.046875 to 0.046875
- adapter_second_factor: bfloat16 [64, 8192], replicated, may hold values from -0.0625 to 0.0625
- kept_hidden_rows: bfloat16 [1536, 14336], P('dp', 'seq'), may hold values from -6 to 6
- kept_row_index: int32 [1536], P('dp'), may hold values from 0 to 767, as said below
- kept_row_count: int32 [8], P('dp'), may hold values from 1 to 192, 768 in all
- kept_row_scale: float32 [1536], P('dp'), may hold values from 1 to 8
Outputs:
- hidden_gradient: bfloat16 [6144, 14336], P('dp', 'seq')
- first_factor_gradient: float32 [14336, 64], P('seq')
- second_factor_gradient: float32 [64, 8192], P(None, ('dp', 'seq'))
The draws below stay inside these ranges and needn't reach their ends.
Inputs may be any that keep to these rules, and one draw needn't show every extreme that they name: `kept_row_index`: within each aligned block of 192 entries (one dp index) the entries are distinct; only the first kept_row_count entries of a block are valid.
All inputs are finite; a program needn't handle non-finite values. No bound on the sum of `kept_row_count` on one device may be relied on, other than what follows from the above.
Results may differ from the reference program's by a relative error of at most 0.0051.
Values may be sent and summed in bfloat16 or wider, within the bound.
A program may use at most 192 MiB of HBM per device.

```python
import math
import jax
import jax.numpy as jnp
import numpy as np
from jax import lax

MODEL_WIDTH = 8192
HIDDEN_UNITS = 14336
ADAPTER_RANK = 64
TOKENS_PER_SHARD = 768
TOKENS = 6144
KCAP = 192
KEPT = 1536
N_DP = 8


def draw_kept_row_index(key, part):
    keys = jax.random.split(key, N_DP)

    def one_block(block_key):
        first_key, second_key = jax.random.split(block_key)
        inner = jax.random.permutation(first_key, TOKENS_PER_SHARD - 2).astype(jnp.int32) + 1
        ends = jnp.array([0, TOKENS_PER_SHARD - 1], dtype=jnp.int32)
        chosen = jnp.concatenate([ends, inner[:KCAP - 2]])
        return jax.random.permutation(second_key, chosen)
    return jax.vmap(one_block)(keys).reshape(-1).astype(jnp.int32)


def with_spikes(values, own_key, source, target, shards_of, factor):
    owner, partner = [(jnp.arange(values.shape[axis_at]) // (values.shape[axis_at] // shards_of)).reshape([-1 if axis == axis_at else 1 for axis in range(values.ndim)]) for axis_at in (source, target)]
    chosen = jax.random.permutation(own_key, shards_of)[partner]
    strong = (owner == chosen) | (owner == (partner + shards_of // 2) % shards_of)
    return jnp.where(strong, factor * values, values)


def block_scale(own_key, extent, cuts, smallest, high):
    level = 1.0
    for axis_at, parts in cuts:
        draws = jax.random.uniform(jax.random.fold_in(jax.random.fold_in(own_key, 6), axis_at), (parts,), jnp.float32, smallest / len(cuts), high / len(cuts))
        level = level * jnp.repeat(jnp.exp(draws), extent[axis_at] // parts).reshape((-1,) + (1,) * (len(extent) - 1 - axis_at))
    return level


def length_profile(count, total, limit, lean):
    portions = [(1 << 20) // math.isqrt(standing ** lean) + 1 for standing in range(2, count + 1)]
    rest, holding = total - limit - (count - 1), [1] * (count - 1)
    while rest > 0:
        candidates = [i for i in range(count - 1) if holding[i] < limit]
        mass, budget = sum([portions[i] for i in candidates]), rest
        for i in candidates:
            addition = min(limit - holding[i], max(1, budget * portions[i] // mass), rest)
            holding[i] = holding[i] + addition
            rest = rest - addition
    return np.array([limit] + holding)


def uneven(rng, amount, total, reach, slope):
    if amount == 2:
        one = jax.random.randint(rng, (), max(1, total - reach), min(reach, total - 1) + 1)
        return jnp.stack([one, total - one])
    tallies = jnp.asarray(length_profile(amount, total, reach, slope), jnp.int32)
    pairs = (amount - 1) // 2
    source_of, taker = tallies[1:1 + 2 * pairs:2], tallies[2:2 + 2 * pairs:2]
    slack = jnp.minimum(source_of - 1, reach - taker)
    passed = jax.random.randint(jax.random.fold_in(rng, 1), (pairs,), 0, 1 << 20) % (slack + 1)
    tallies = tallies.at[1:1 + 2 * pairs:2].set(source_of - passed).at[2:2 + 2 * pairs:2].set(taker + passed)
    return tallies[jax.random.permutation(jax.random.fold_in(rng, 2), amount)]


def centred(stream_key, extent, width, limit, cuts=(), held_as=jnp.bfloat16):
    result = width * jax.random.normal(stream_key, extent, jnp.float32)
    if cuts:
        result = result * block_scale(stream_key, extent, cuts, -0.22, 0.18)
    return jnp.clip(result, -limit, limit).astype(held_as)


def bell_draw_with(key, extent, scale, bound, shards, heavy, held_as=jnp.bfloat16):
    result = scale * jax.random.normal(key, extent, jnp.float32)
    if shards:
        result = result * block_scale(key, extent, shards, -0.22, 0.18)
    return jnp.clip(with_spikes(result, jax.random.fold_in(key, 3), *heavy), -bound, bound).astype(held_as)


def setup_inputs(seed: int = 0) -> dict:
    key_list = jax.random.split(jax.random.key(seed), 9)
    return {
        "output_gradient": bell_draw_with(key_list[0], (TOKENS, MODEL_WIDTH), 1.0, 6.0, ((0, 8),), (0, 1, 8, 2.0)),
        "frozen_down_weight": centred(key_list[1], (HIDDEN_UNITS, MODEL_WIDTH), HIDDEN_UNITS ** -0.5, 0.046875, ((0, 4), (1, 8))),
        "adapter_first_factor": centred(key_list[2], (HIDDEN_UNITS, ADAPTER_RANK), HIDDEN_UNITS ** -0.5, 0.046875, ((0, 4),)),
        "adapter_second_factor": centred(key_list[3], (ADAPTER_RANK, MODEL_WIDTH), MODEL_WIDTH ** -0.5, 0.0625),
        "kept_hidden_rows": centred(key_list[4], (KEPT, HIDDEN_UNITS), 1.0, 6.0, ((0, 8), (1, 4))),
        "kept_row_index": draw_kept_row_index(jax.random.fold_in(key_list[8], 71), 0),
        "kept_row_count": uneven(key_list[6], N_DP, N_DP * KCAP // 2, KCAP, 2).astype(jnp.int32),
        "kept_row_scale": jnp.clip(jnp.exp(math.log(8.0) - 2.0794415 * jax.random.uniform(key_list[7], (KEPT,), jnp.float32) ** block_scale(key_list[7], (KEPT,), ((0, 8),), -0.2, 0.2)), 1.0, 8.0),
    }


adapter_scale = 2.0


def reference(output_gradient, frozen_down_weight, adapter_first_factor, adapter_second_factor, kept_hidden_rows, kept_row_index, kept_row_count, kept_row_scale):
    contract_dims = (((1,), (1,)), ((), ()))
    adapter_gradient = lax.dot_general(output_gradient, adapter_second_factor, contract_dims, preferred_element_type=jnp.float32).astype(jnp.bfloat16)
    frozen_product = lax.dot_general(output_gradient, frozen_down_weight, contract_dims, preferred_element_type=jnp.float32)
    adapter_contribution = lax.dot_general(adapter_gradient, adapter_first_factor, contract_dims, preferred_element_type=jnp.float32)
    hidden_gradient = (frozen_product + adapter_scale * adapter_contribution).astype(jnp.bfloat16)
    offsets = (jnp.arange(N_DP, dtype=jnp.int32) * TOKENS_PER_SHARD)[:, None]
    row_positions = (kept_row_index.reshape(N_DP, KCAP).astype(jnp.int32) + offsets).reshape(-1)
    slots = jnp.arange(KCAP, dtype=jnp.int32)[None, :]
    valid = (slots < kept_row_count.astype(jnp.int32)[:, None]).astype(jnp.float32).reshape(-1)
    weight_rows = kept_row_scale * valid
    gradient_kept_rows = jnp.take(adapter_gradient, row_positions, axis=0)
    effective_weight = (weight_rows[:, None] * gradient_kept_rows.astype(jnp.float32)).astype(jnp.bfloat16)
    first_factor_out = (((0,), (0,)), ((), ()))
    first_factor_gradient = lax.dot_general(kept_hidden_rows, effective_weight, first_factor_out, preferred_element_type=jnp.float32) * (adapter_scale / TOKENS_PER_SHARD)
    hidden_kept_rows = jnp.dot(kept_hidden_rows, adapter_first_factor, preferred_element_type=jnp.float32)
    output_gradient_kept = jnp.take(output_gradient, row_positions, axis=0).astype(jnp.float32)
    scaled_gradient_rows = weight_rows[:, None] * hidden_kept_rows
    second_factor_gradient = lax.dot_general(scaled_gradient_rows, output_gradient_kept, first_factor_out, precision=lax.Precision.HIGHEST, preferred_element_type=jnp.float32) * (adapter_scale / TOKENS_PER_SHARD)
    return hidden_gradient, first_factor_gradient, second_factor_gradient
```

```python
import functools

import jax
import jax.numpy as jnp
from jax import lax
from jax.experimental import pallas as pl
from jax.experimental.pallas import tpu as pltpu
from jax.sharding import PartitionSpec as P

adapter_scale = 2.0
MESH = pl.DeviceIdType.MESH
GROUP = 4
AHEAD = 8
RELAY = 4
LAG = 4
BUFS = 4


def nt(a, b):
    return lax.dot_general(a, b, (((1,), (1,)), ((), ())), preferred_element_type=jnp.float32)


def hidden_kernel(
    n_rs, n_seq, tile, og, w, lora_g, first, out,
    slots, acts, part_in, part_out, staged,
    s1s, s1r, s2s, s2r, s3s, s3r, pss, psr, axs, axr, bcs, bcr, loc, outs,
):
    d, s = lax.axis_index("dp"), lax.axis_index("seq")
    hi, lo = d // GROUP, lax.rem(d, GROUP)
    chunks = w.shape[0] // tile
    width = w.shape[1]
    tokens = og.shape[0]
    quarter = tokens // n_seq

    def xor(value, bits):
        result = value
        step = 1
        while step <= bits:
            if bits & step:
                result = result + step - 2 * step * lax.rem(result // step, 2)
            step *= 2
        return result

    px, pz = (xor(d, 1), s), (xor(d, 2), s)
    partners = [(xor(hi, r) * GROUP + lo, s) for r in range(1, n_rs)]
    peers = [(d, xor(s, q)) for q in range(1, n_seq)]

    barrier = pltpu.get_barrier_semaphore()
    for other in [px, pz] + partners + peers:
        pl.semaphore_signal(barrier, inc=1, device_id=other, device_id_type=MESH)
    pl.semaphore_wait(barrier, 2 + len(partners) + len(peers))

    def rows(c):
        return pl.ds(pl.multiple_of(c * tile, tile), tile)

    def remote(src, dst, send, recv, device):
        return pltpu.make_async_remote_copy(
            src_ref=src, dst_ref=dst, send_sem=send, recv_sem=recv,
            device_id=device, device_id_type=MESH,
        )

    def own_x(c):
        return remote(w.at[rows(c)], slots.at[1, rows(c)], s1s.at[c], s1r.at[c], px)

    def own_z(c):
        return remote(w.at[rows(c)], slots.at[2, rows(c)], s2s.at[c], s2r.at[c], pz)

    def relay(c):
        return remote(slots.at[2, rows(c)], slots.at[3, rows(c)], s3s.at[c], s3r.at[c], px)

    def partial(r, c):
        return remote(
            part_out.at[r, lax.rem(c, BUFS)], part_in.at[r, c], pss.at[r, c], psr.at[r, c], partners[r]
        )

    my_rows = pl.ds(pl.multiple_of(s * quarter, quarter), quarter)

    def columns(group, j):
        return pl.ds(pl.multiple_of((group * GROUP + xor(lo, j)) * width, width), width)

    def exchange(r, j):
        return remote(
            og.at[my_rows, columns(xor(hi, r + 1), j)], acts.at[r + 1, j, my_rows],
            axs.at[r, j], axr.at[r, j], partners[r],
        )

    def spread(r, j, q):
        return remote(
            acts.at[r + 1, j, my_rows], acts.at[r + 1, j, my_rows],
            bcs.at[r, j, q], bcr.at[r, j, q], peers[q],
        )

    local = [pltpu.make_async_copy(w, slots.at[0], loc.at[GROUP])]
    for j in range(GROUP):
        local.append(pltpu.make_async_copy(og.at[:, columns(hi, j)], acts.at[0, j], loc.at[j]))

    for j in range(GROUP):
        for r in range(n_rs - 1):
            exchange(r, j).start()
    ahead = min(AHEAD, chunks)
    relayed = min(RELAY, chunks)

    @pl.loop(0, ahead)
    def _(c):
        own_z(c).start()
        own_x(c).start()

    for copy in local:
        copy.start()
    for j in range(GROUP):
        for r in range(n_rs - 1):
            exchange(r, j).wait_recv()
            for q in range(n_seq - 1):
                spread(r, j, q).start()
        if j < relayed:
            own_z(j).wait_recv()
            relay(j).start()
    for copy in local:
        copy.wait()
    for j in range(GROUP):
        for r in range(n_rs - 1):
            for q in range(n_seq - 1):
                spread(r, j, q).wait_recv()

    def product(b, c):
        total = nt(acts[b, 0], slots[0, rows(c)])
        for j in range(1, GROUP):
            total += nt(acts[b, j], slots[j, rows(c)])
        return total

    def store(c):
        at = lax.rem(c, 2)
        return pltpu.make_async_copy(
            staged.at[at], out.at[:, rows(c)], outs.at[at]
        )

    lag = min(LAG, chunks)

    @pl.loop(0, chunks + lag)
    def _(c):
        @pl.when(c + ahead < chunks)
        def _():
            own_z(c + ahead).start()
            own_x(c + ahead).start()

        @pl.when(c + relayed < chunks)
        def _():
            own_z(c + relayed).wait_recv()
            relay(c + relayed).start()

        @pl.when(c < chunks)
        def _():
            own_x(c).wait_recv()
            relay(c).wait_recv()
            for r in range(n_rs - 1):
                @pl.when(c >= BUFS)
                def _():
                    partial(r, c - BUFS).wait_send()
                part_out[r, lax.rem(c, BUFS)] = product(r + 1, c).astype(jnp.bfloat16)
                partial(r, c).start()

        @pl.when(c >= lag)
        def _():
            f = c - lag
            total = product(0, f) + adapter_scale * nt(lora_g[...], first[rows(f)])
            for r in range(n_rs - 1):
                partial(r, f).wait_recv()
                total += part_in[r, f].astype(jnp.float32)

            @pl.when(f >= 2)
            def _():
                store(f - 2).wait()
            staged[lax.rem(f, 2)] = total.astype(jnp.bfloat16)
            store(f).start()

    for f in range(max(chunks - 2, 0), chunks):
        store(f).wait()

    @pl.loop(0, chunks)
    def _(c):
        own_x(c).wait_send()
        own_z(c).wait_send()
        relay(c).wait_send()

    for r in range(n_rs - 1):
        for f in range(max(chunks - BUFS, 0), chunks):
            partial(r, f).wait_send()
        for j in range(GROUP):
            exchange(r, j).wait_send()
            for q in range(n_seq - 1):
                spread(r, j, q).wait_send()


def hidden(n_dp, n_seq, og, w, lora_g, first):
    tokens, hidden_rows, width = og.shape[0], w.shape[0], w.shape[1]
    n_rs = n_dp // GROUP
    tile = next(t for t in (256, 128) if hidden_rows % t == 0)
    chunks = hidden_rows // tile
    dma = pltpu.SemaphoreType.DMA
    bf16 = jnp.bfloat16
    others = n_rs - 1
    return pl.pallas_call(
        functools.partial(hidden_kernel, n_rs, n_seq, tile),
        out_shape=jax.ShapeDtypeStruct((tokens, hidden_rows), bf16),
        in_specs=[
            pl.BlockSpec(memory_space=pl.ANY),
            pl.BlockSpec(memory_space=pl.ANY),
            pl.BlockSpec(memory_space=pltpu.VMEM),
            pl.BlockSpec(memory_space=pltpu.VMEM),
        ],
        out_specs=pl.BlockSpec(memory_space=pl.ANY),
        scratch_shapes=[
            pltpu.VMEM((GROUP, hidden_rows, width), bf16),
            pltpu.VMEM((n_rs, GROUP, tokens, width), bf16),
            pltpu.VMEM((others, chunks, tokens, tile), bf16),
            pltpu.VMEM((others, BUFS, tokens, tile), bf16),
            pltpu.VMEM((2, tokens, tile), bf16),
            dma((chunks,)), dma((chunks,)), dma((chunks,)),
            dma((chunks,)), dma((chunks,)), dma((chunks,)),
            dma((others, chunks)), dma((others, chunks)),
            dma((others, GROUP)), dma((others, GROUP)),
            dma((others, GROUP, n_seq - 1)), dma((others, GROUP, n_seq - 1)),
            dma((GROUP + 1,)), dma((2,)),
        ],
        compiler_params=pltpu.CompilerParams(
            collective_id=0, has_side_effects=True, vmem_limit_bytes=62 * 1024 * 1024
        ),
        cost_estimate=pl.CostEstimate(
            flops=2 * tokens * hidden_rows * width * n_dp,
            bytes_accessed=og.size * 2 + w.size * 2 * GROUP, transcendentals=0,
        ),
    )(og, w, lora_g, first)


def on_device(
    n_dp,
    n_seq,
    output_gradient,
    frozen_down_weight,
    adapter_first_factor,
    adapter_second_factor,
    kept_hidden_rows,
    kept_row_index,
    kept_row_count,
    kept_row_scale,
):
    contract_dims = (((1,), (1,)), ((), ()))
    first_factor_out = (((0,), (0,)), ((), ()))
    token_rows = output_gradient.shape[0]
    adapter_gradient = lax.dot_general(
        output_gradient, adapter_second_factor, contract_dims, preferred_element_type=jnp.float32
    ).astype(jnp.bfloat16)
    hidden_gradient = hidden(
        n_dp, n_seq, output_gradient, frozen_down_weight, adapter_gradient, adapter_first_factor
    )
    slots = kept_row_index.shape[0]
    valid = (jnp.arange(slots, dtype=jnp.int32) < kept_row_count[0]).astype(jnp.float32)
    weight_rows = kept_row_scale * valid
    gradient_kept_rows = jnp.take(adapter_gradient, kept_row_index, axis=0)
    w_rows = (weight_rows[:, None] * gradient_kept_rows.astype(jnp.float32)).astype(jnp.bfloat16)
    part_a = lax.dot_general(
        kept_hidden_rows, w_rows, first_factor_out, preferred_element_type=jnp.float32
    ) * (adapter_scale / token_rows)
    first_factor_gradient = lax.psum(part_a, "dp")
    output_gradient_kept = jnp.take(output_gradient, kept_row_index, axis=0)
    partial_hidden_gradient = jnp.dot(
        kept_hidden_rows, adapter_first_factor, preferred_element_type=jnp.float32
    )
    scaled_gradient_rows = weight_rows[:, None] * partial_hidden_gradient
    chosen = output_gradient_kept.astype(jnp.float32)
    term_b = lax.dot_general(
        scaled_gradient_rows,
        chosen,
        first_factor_out,
        precision=lax.Precision.HIGHEST,
        preferred_element_type=jnp.float32,
    ) * (adapter_scale / token_rows)
    second_factor_gradient = lax.psum_scatter(
        term_b, ("dp", "seq"), scatter_dimension=1, tiled=True
    )
    return (hidden_gradient, first_factor_gradient, second_factor_gradient)


def solution(mesh):
    in_specs = (
        P("dp", None),
        P("seq", "dp"),
        P("seq", None),
        P(),
        P("dp", "seq"),
        P("dp"),
        P("dp"),
        P("dp"),
    )
    out_specs = (P("dp", "seq"), P("seq", None), P(None, ("dp", "seq")))
    return jax.shard_map(
        functools.partial(on_device, mesh.shape["dp"], mesh.shape["seq"]),
        mesh=mesh, in_specs=in_specs, out_specs=out_specs, check_vma=False
    )
```

```python
import functools

import jax
import jax.numpy as jnp
from jax import lax
from jax.experimental import pallas as pl
from jax.experimental.pallas import tpu as pltpu
from jax.sharding import PartitionSpec as P

adapter_scale = 2.0
MESH = pl.DeviceIdType.MESH
GROUP = 4
AHEAD = 8
RELAY = 4
LAG = 4
VMEM_BYTES = 63 * 1024 * 1024
BUFS = 3


def nt(a, b):
    return lax.dot_general(a, b, (((1,), (1,)), ((), ())), preferred_element_type=jnp.float32)


def tn(a, b):
    return lax.dot_general(a, b, (((0,), (0,)), ((), ())), preferred_element_type=jnp.float32)


def hidden_kernel(
    n_dp, n_seq, tile, og, w, first, second, kept, index, scale, count, out, first_out, second_out,
    slots, acts, part_in, part_out, staged, stream, lora_g, terms, terms_in, sums, sums_in,
    pieces, pieces_in, whole,
    s1s, s1r, s2s, s2r, s3s, s3r, pss, psr, axs, axr, bcs, bcr, loc, outs, strs,
    tss, tsr, uss, usr, vss, vsr, wss, wsr,
):
    n_rs = n_dp // GROUP
    d, s = lax.axis_index("dp"), lax.axis_index("seq")
    hi, lo = d // GROUP, lax.rem(d, GROUP)
    chunks = w.shape[0] // tile
    width = w.shape[1]
    tokens = og.shape[0]
    quarter = tokens // n_seq

    def xor(value, bits):
        result = value
        step = 1
        while step <= bits:
            if bits & step:
                result = result + step - 2 * step * lax.rem(result // step, 2)
            step *= 2
        return result

    px, pz = (xor(d, 1), s), (xor(d, 2), s)
    partners = [(xor(hi, r) * GROUP + lo, s) for r in range(1, n_rs)]
    peers = [(d, xor(s, q)) for q in range(1, n_seq)]

    group_peers = [(xor(d, k), s) for k in range(1, n_dp)]

    barrier = pltpu.get_barrier_semaphore()
    for other in group_peers + peers:
        pl.semaphore_signal(barrier, inc=1, device_id=other, device_id_type=MESH)
    pl.semaphore_wait(barrier, len(group_peers) + len(peers))

    def rows(c):
        return pl.ds(pl.multiple_of(c * tile, tile), tile)

    def remote(src, dst, send, recv, device):
        return pltpu.make_async_remote_copy(
            src_ref=src, dst_ref=dst, send_sem=send, recv_sem=recv,
            device_id=device, device_id_type=MESH,
        )

    def own_x(c):
        return remote(w.at[rows(c)], slots.at[1, rows(c)], s1s.at[c], s1r.at[c], px)

    def own_z(c):
        return remote(w.at[rows(c)], slots.at[2, rows(c)], s2s.at[c], s2r.at[c], pz)

    def relay(c):
        return remote(slots.at[2, rows(c)], slots.at[3, rows(c)], s3s.at[c], s3r.at[c], px)

    def partial(r, c):
        return remote(
            part_out.at[r, lax.rem(c, BUFS)], part_in.at[r, c], pss.at[r, c], psr.at[r, c], partners[r]
        )

    my_rows = pl.ds(pl.multiple_of(s * quarter, quarter), quarter)

    def columns(group, j):
        return pl.ds(pl.multiple_of((group * GROUP + xor(lo, j)) * width, width), width)

    def exchange(r, j):
        return remote(
            og.at[my_rows, columns(xor(hi, r + 1), j)], acts.at[r + 1, j, my_rows],
            axs.at[r, j], axr.at[r, j], partners[r],
        )

    def spread(r, j, q):
        return remote(
            acts.at[r + 1, j, my_rows], acts.at[r + 1, j, my_rows],
            bcs.at[r, j, q], bcr.at[r, j, q], peers[q],
        )

    local = [pltpu.make_async_copy(w, slots.at[0], loc.at[GROUP])]
    for j in range(GROUP):
        local.append(pltpu.make_async_copy(og.at[:, columns(hi, j)], acts.at[0, j], loc.at[j]))

    for j in range(GROUP):
        for r in range(n_rs - 1):
            exchange(r, j).start()
    ahead = min(AHEAD, chunks)
    relayed = min(RELAY, chunks)

    @pl.loop(0, ahead)
    def _(c):
        own_z(c).start()
        own_x(c).start()

    for copy in local[1:] + local[:1]:
        copy.start()

    others = [(r, j) for j in range(GROUP) for r in range(1, n_rs)]

    def streamed(at):
        r, j = others[at]
        return pltpu.make_async_copy(
            og.at[:, columns(xor(hi, r), j)], stream, strs.at[at]
        )

    if others:
        streamed(0).start()

    kept_slots = index.shape[1]
    factor = adapter_scale / tokens
    picks = (
        lax.broadcasted_iota(jnp.int32, (tokens, kept_slots), 0) == index[...]
    ).astype(jnp.float32).astype(jnp.bfloat16)
    valid = lax.broadcasted_iota(jnp.int32, (1, kept_slots), 1) < count[0]
    weights_row = jnp.where(valid, scale[...], 0.0)
    diagonal = lax.broadcasted_iota(jnp.int32, (kept_slots, kept_slots), 0) == (
        lax.broadcasted_iota(jnp.int32, (kept_slots, kept_slots), 1)
    )
    weights = jnp.sum(jnp.where(diagonal, weights_row, 0.0), axis=1, keepdims=True)
    kept_h = nt(kept[...], first[...])
    scaled = weights * kept_h
    scaled_high = scaled.astype(jnp.bfloat16)
    scaled_low = (scaled - scaled_high.astype(jnp.float32)).astype(jnp.bfloat16)
    cut = width // n_seq

    def side(block, r, j, total):
        at = xor(hi, r) * GROUP + xor(lo, j)
        span = pl.ds(pl.multiple_of(at * width, width), width)
        chosen = tn(picks, block).astype(jnp.bfloat16)
        term = (tn(scaled_high, chosen) + tn(scaled_low, chosen)) * factor
        for q in range(n_seq):
            terms[q, at] = term[:, q * cut : (q + 1) * cut].astype(jnp.bfloat16)
        return total + nt(block, second[:, span])

    def gather_terms(q):
        return remote(terms.at[xor(s, q)], terms_in.at[q - 1], tss.at[q - 1], tsr.at[q - 1], peers[q - 1])

    def reduce_terms(k):
        return remote(sums.at[xor(d, k)], sums_in.at[k - 1], uss.at[k - 1], usr.at[k - 1], group_peers[k - 1])

    def reduce_first(k):
        return remote(pieces.at[xor(d, k)], pieces_in.at[k - 1], vss.at[k - 1], vsr.at[k - 1], group_peers[k - 1])

    def gather_first(k):
        return remote(whole.at[d], whole.at[d], wss.at[k - 1], wsr.at[k - 1], group_peers[k - 1])

    def landed_first(k):
        at = xor(d, k)
        return remote(whole.at[at], whole.at[at], wss.at[k - 1], wsr.at[k - 1], group_peers[k - 1])

    total = jnp.zeros(lora_g.shape, jnp.float32)
    for j in range(GROUP):
        local[1 + j].wait()
        total = side(acts[0, j], 0, j, total)
        for r in range(1, n_rs):
            at = others.index((r, j))
            streamed(at).wait()
            total = side(stream[...], r, j, total)
            if at + 1 < len(others):
                streamed(at + 1).start()
        for r in range(n_rs - 1):
            exchange(r, j).wait_recv()
            for q in range(n_seq - 1):
                spread(r, j, q).start()
        if j < relayed:
            own_z(j).wait_recv()
            relay(j).start()
    for q in range(1, n_seq):
        gather_terms(q).start()
    lora_g[...] = total.astype(jnp.bfloat16)
    w_rows = (weights * tn(picks, lora_g[...])).astype(jnp.bfloat16)
    half = w.shape[0] // 2
    both = jnp.concatenate([tn(kept[:, :half], w_rows), tn(kept[:, half:], w_rows)], axis=1)
    pieces[...] = (both * factor).astype(jnp.bfloat16).reshape(pieces.shape)
    for k in range(1, n_dp):
        reduce_first(k).start()
    local[0].wait()
    for j in range(GROUP):
        for r in range(n_rs - 1):
            for q in range(n_seq - 1):
                spread(r, j, q).wait_recv()

    def product(b, c):
        total = nt(acts[b, 0], slots[0, rows(c)])
        for j in range(1, GROUP):
            total += nt(acts[b, j], slots[j, rows(c)])
        return total

    def store(c):
        at = lax.rem(c, 2)
        return pltpu.make_async_copy(
            staged.at[at], out.at[:, rows(c)], outs.at[at]
        )

    lag = min(LAG, chunks)

    @pl.loop(0, chunks + lag)
    def _(c):
        @pl.when(c == chunks // 4)
        def _():
            for q in range(1, n_seq):
                gather_terms(q).wait_recv()
            for b in range(n_dp):
                part = terms[s, b].astype(jnp.float32)
                for q in range(1, n_seq):
                    part += terms_in[q - 1, b].astype(jnp.float32)
                sums[b] = part.astype(jnp.bfloat16)
            for k in range(1, n_dp):
                reduce_terms(k).start()
                reduce_first(k).wait_recv()
            part = pieces[d].astype(jnp.float32)
            for k in range(1, n_dp):
                part += pieces_in[k - 1].astype(jnp.float32)
            whole[d] = part.astype(jnp.bfloat16)
            for k in range(1, n_dp):
                gather_first(k).start()

        @pl.when(c == chunks // 2)
        def _():
            for k in range(1, n_dp):
                reduce_terms(k).wait_recv()
                landed_first(k).wait_recv()
            part = sums[d].astype(jnp.float32)
            for k in range(1, n_dp):
                part += sums_in[k - 1].astype(jnp.float32)
            second_out[...] = part
            values = whole[...].astype(jnp.float32).reshape(half, whole.shape[2]).T
            first_out[:, :half] = values[: first.shape[0]]
            first_out[:, half:] = values[first.shape[0] :]

        @pl.when(c + ahead < chunks)
        def _():
            own_z(c + ahead).start()
            own_x(c + ahead).start()

        @pl.when(c + relayed < chunks)
        def _():
            own_z(c + relayed).wait_recv()
            relay(c + relayed).start()

        @pl.when(c < chunks)
        def _():
            own_x(c).wait_recv()
            relay(c).wait_recv()
            for r in range(n_rs - 1):
                @pl.when(c >= BUFS)
                def _():
                    partial(r, c - BUFS).wait_send()
                part_out[r, lax.rem(c, BUFS)] = product(r + 1, c).astype(jnp.bfloat16)
                partial(r, c).start()

        @pl.when(c >= lag)
        def _():
            f = c - lag
            total = product(0, f) + adapter_scale * jnp.dot(
                lora_g[...], first[:, rows(f)], preferred_element_type=jnp.float32
            )
            for r in range(n_rs - 1):
                partial(r, f).wait_recv()
                total += part_in[r, f].astype(jnp.float32)

            @pl.when(f >= 2)
            def _():
                store(f - 2).wait()
            staged[lax.rem(f, 2)] = total.astype(jnp.bfloat16)
            store(f).start()

    for f in range(max(chunks - 2, 0), chunks):
        store(f).wait()

    @pl.loop(0, chunks)
    def _(c):
        own_x(c).wait_send()
        own_z(c).wait_send()
        relay(c).wait_send()

    for q in range(1, n_seq):
        gather_terms(q).wait_send()
    for k in range(1, n_dp):
        reduce_terms(k).wait_send()
        reduce_first(k).wait_send()
        gather_first(k).wait_send()
    for r in range(n_rs - 1):
        for f in range(max(chunks - BUFS, 0), chunks):
            partial(r, f).wait_send()
        for j in range(GROUP):
            exchange(r, j).wait_send()
            for q in range(n_seq - 1):
                spread(r, j, q).wait_send()


def on_device(n_dp, n_seq, og, w, first, second, kept, index, count, scale):
    tokens, hidden_rows, width = og.shape[0], w.shape[0], w.shape[1]
    rank = second.shape[0]
    n_rs = n_dp // GROUP
    tile = next(t for t in (256, 128) if hidden_rows % t == 0)
    chunks = hidden_rows // tile
    cut = second.shape[1] // (n_dp * n_seq)
    piece = hidden_rows // (2 * n_dp)
    dma = pltpu.SemaphoreType.DMA
    bf16 = jnp.bfloat16
    others = n_rs - 1
    anywhere = pl.BlockSpec(memory_space=pl.ANY)
    vmem = pl.BlockSpec(memory_space=pltpu.VMEM)
    smem = pl.BlockSpec(memory_space=pltpu.SMEM)
    hidden_gradient, first_gradient, second_gradient = pl.pallas_call(
        functools.partial(hidden_kernel, n_dp, n_seq, tile),
        out_shape=(
            jax.ShapeDtypeStruct((tokens, hidden_rows), bf16),
            jax.ShapeDtypeStruct((rank, hidden_rows), jnp.float32),
            jax.ShapeDtypeStruct((rank, cut), jnp.float32),
        ),
        in_specs=[anywhere, anywhere, vmem, vmem, vmem, vmem, vmem, smem],
        out_specs=(anywhere, vmem, vmem),
        scratch_shapes=[
            pltpu.VMEM((GROUP, hidden_rows, width), bf16),
            pltpu.VMEM((n_rs, GROUP, tokens, width), bf16),
            pltpu.VMEM((others, chunks, tokens, tile), bf16),
            pltpu.VMEM((others, BUFS, tokens, tile), bf16),
            pltpu.VMEM((2, tokens, tile), bf16),
            pltpu.VMEM((tokens, width), bf16),
            pltpu.VMEM((tokens, rank), bf16),
            pltpu.VMEM((n_seq, n_dp, rank, cut), bf16),
            pltpu.VMEM((n_seq - 1, n_dp, rank, cut), bf16),
            pltpu.VMEM((n_dp, rank, cut), bf16),
            pltpu.VMEM((n_dp - 1, rank, cut), bf16),
            pltpu.VMEM((n_dp, piece, 2 * rank), bf16),
            pltpu.VMEM((n_dp - 1, piece, 2 * rank), bf16),
            pltpu.VMEM((n_dp, piece, 2 * rank), bf16),
            dma((chunks,)), dma((chunks,)), dma((chunks,)),
            dma((chunks,)), dma((chunks,)), dma((chunks,)),
            dma((others, chunks)), dma((others, chunks)),
            dma((others, GROUP)), dma((others, GROUP)),
            dma((others, GROUP, n_seq - 1)), dma((others, GROUP, n_seq - 1)),
            dma((GROUP + 1,)), dma((2,)), dma((others * GROUP,)),
            dma((n_seq - 1,)), dma((n_seq - 1,)), dma((n_dp - 1,)), dma((n_dp - 1,)),
            dma((n_dp - 1,)), dma((n_dp - 1,)), dma((n_dp - 1,)), dma((n_dp - 1,)),
        ],
        compiler_params=pltpu.CompilerParams(
            collective_id=0, has_side_effects=True, vmem_limit_bytes=VMEM_BYTES
        ),
        cost_estimate=pl.CostEstimate(
            flops=2 * tokens * hidden_rows * width * n_dp,
            bytes_accessed=og.size * 2 + w.size * 2 * GROUP, transcendentals=0,
        ),
    )(og, w, first.T, second, kept, index.reshape(1, -1), scale.reshape(1, -1), count)
    return hidden_gradient, first_gradient.T, second_gradient


def solution(mesh):
    in_specs = (
        P("dp", None),
        P("seq", "dp"),
        P("seq", None),
        P(),
        P("dp", "seq"),
        P("dp"),
        P("dp"),
        P("dp"),
    )
    out_specs = (P("dp", "seq"), P("seq", None), P(None, ("dp", "seq")))
    return jax.shard_map(
        functools.partial(on_device, mesh.shape["dp"], mesh.shape["seq"]),
        mesh=mesh, in_specs=in_specs, out_specs=out_specs, check_vma=False
    )
```
